32 devices in a mesh: group: 2 (over y), lat: 4 (over z), lon: 2 (over x), sub: 2 (over core).
Axes of the slice: x: 2, y: 2, z: 4, core: 2. Of those that a mesh axis runs over, the one named last changes fastest.
Arguments:
- grid_latent: bfloat16 [8192, 512], P(('group', 'lat', 'lon', 'sub')), parts along dimension 0, may hold values from -6 to 6
- grid_band: int32 [8192, 1], P(('group', 'lat', 'lon', 'sub')), parts along dimension 0, may hold values from 0 to 3; in each aligned block of 256 rows (0 to 255, 256 to 511, ...) at most 128 rows name the same one
- edge_rows: int32 [8192, 2], P(('group', 'lat', 'lon', 'sub')), parts along dimension 0, may hold values from 0 to 63
- mesh_latent: bfloat16 [1024, 512], P(('group', 'lat', 'lon')), parts along dimension 0, may hold values from -6 to 6
- mesh_slots: int32 [1024, 8], P(('group', 'lat', 'lon'), 'sub'), parts along dimension 0, may hold values from 0 to 191, as said below
- send_rows: int32 [16, 8, 16], P(('group', 'lat', 'lon')), parts along dimension 0, may hold values from 0 to 63
- enc_send: bfloat16 [512, 512], replicated, may hold values from -0.25 to 0.25
- enc_recv: bfloat16 [512, 512], replicated, may hold values from -0.25 to 0.25
- enc_edge: bfloat16 [512, 512], replicated, may hold values from -0.25 to 0.25
- bias_grid: float32 [512], replicated, may hold values from -4 to 4
- node_gain: float32 [512], replicated, may hold values from 0.1 to 1.9
- proc_send: bfloat16 [512, 512], replicated, may hold values from -0.25 to 0.25
- proc_recv: bfloat16 [512, 512], replicated, may hold values from -0.25 to 0.25
- proc_edge: bfloat16 [512, 512], replicated, may hold values from -0.25 to 0.25
- bias_mesh: float32 [512], replicated, may hold values from -4 to 4
- mesh_gain: float32 [512], replicated, may hold values from 0.1 to 1.9
- cotangent: bfloat16 [1024, 512], P(('group', 'lat', 'lon')), parts along dimension 0, may hold values from -6 to 6
Outputs:
- mesh_out: bfloat16 [1024, 512], P(('group', 'lat', 'lon')), parts along dimension 0
- mesh_grad: bfloat16 [1024, 512], P(('group', 'lat', 'lon')), parts along dimension 0
- grid_grad: bfloat16 [8192, 512], P(('group', 'lat', 'lon', 'sub')), parts along dimension 0
The draws below stay inside these ranges and needn't reach their ends.
There are 2 independent parts, one for each index of `group`. The reference program is written for one: setup_inputs(seed, part) draws one part's arguments, and reference() takes and returns one part's arrays. A program takes and returns all parts, laid end to end along the dimension named above; an argument that names none is the same for every part. Nothing has to cross between parts.
Inputs may be any that keep to these rules, and one draw needn't show every extreme that they name: `grid_band`: among the grid nodes of one device at most 128 name the same band, and in every draw some device's nodes name one band exactly 128 times. `mesh_slots`: A slot at or above 64 never refers to a band outside 0 to 3.
All inputs are finite; a program needn't handle non-finite values.
Results may differ from the reference program's by a relative error of at most 0.014.
Values may be sent and summed in bfloat16 or wider, within the bound.
A program may use at most 64 MiB of HBM per device.

```python
import math
import jax
import jax.numpy as jnp
import numpy as np
from jax import lax

D = 512
GRID_DEV = 256
MESH_PART = 64
BND = 16
KG = 2
KM = 8
CAP = 128
NPART = 8
GRID = 4096
MESH = 512
N_LAT = 4
N_LON = 2
N_SUB = 2


def draw_mesh_slots(key, part):
    key = jax.random.fold_in(key, 11)
    extent = MESH_PART + 8 * BND
    picked = jax.random.randint(key, (MESH, KM), 0, extent)
    own_band = jnp.arange(MESH, dtype=jnp.int32) // MESH_PART // N_LON
    direction = jnp.clip((picked - MESH_PART) // BND, 0, 7)
    lat_move = jnp.array([-1, -1, -1, 0, 0, 1, 1, 1], dtype=jnp.int32)[direction]
    source = own_band[:, None] - lat_move
    usable = (picked < MESH_PART) | (source >= 0) & (source < N_LAT)
    return jnp.where(usable, picked, picked % MESH_PART).astype(jnp.int32)


def plant(values, rng, least, largest):
    longest = values.shape.index(max(values.shape))
    spots = []
    for shift in (0, 1):
        where = [jax.random.randint(jax.random.fold_in(rng, axis), (), 0, length) for axis, length in enumerate(values.shape)]
        where[longest] = (where[longest] + shift) % values.shape[longest]
        spots.append(tuple(where))
    return values.at[spots[0]].set(least).at[spots[1]].set(largest)


def block_scale(stream_key, shape, shards, least, top_value):
    loudness, own = 1.0, jax.random.fold_in(stream_key, 6)
    for axis_at, parts in shards:
        heights = jnp.exp(jax.random.uniform(jax.random.fold_in(own, axis_at), (parts,), jnp.float32, least / len(shards), top_value / len(shards)))
        loudness = loudness * jnp.repeat(heights, shape[axis_at] // parts).reshape([-1 if axis == axis_at else 1 for axis in range(len(shape))])
    return loudness


def assign_block(own_key, own, number, rows, number_of, top, most, skew):
    sequence = jax.random.permutation(own_key, number_of)
    crowded, ordinary = load_shares(number_of, rows * top, most, skew, True), load_shares(number_of, rows * top, most, skew, False)
    places = jnp.arange(number_of)

    def named(lengths, turn):
        used = int((lengths > 0).sum())
        fixed = max(1, used // 4)
        shifted = fixed + (places - fixed + turn * (used - fixed)) % max(1, number_of - fixed)
        return jnp.zeros((number_of,), jnp.int32).at[sequence[jnp.where(places < fixed, places, shifted)]].set(jnp.asarray(lengths, jnp.int32))

    lengths = jnp.where(number % 4 == 0, named(crowded, number // 4), named(ordinary, number - number // 4 - 1))
    mixed = jax.random.permutation(jax.random.fold_in(own, 3), number_of)
    donor, receiver = mixed[0:number_of // 2 * 2:2], mixed[1:number_of // 2 * 2:2]
    room = jnp.minimum(lengths[donor] - 1, most - lengths[receiver]) // 2
    room = jnp.where((donor == sequence[0]) | (receiver == sequence[0]) | (lengths[receiver] == 0), 0, jnp.maximum(room, 0))
    shifted = jax.random.randint(jax.random.fold_in(own, 4), (number_of // 2,), 0, 1 << 20) % (room + 1)
    lengths = lengths.at[donor].add(-shifted).at[receiver].add(shifted)
    labels = jnp.searchsorted(jnp.cumsum(lengths), jnp.arange(rows * top), side="right").astype(jnp.int32)
    grid = labels.reshape(top, rows).T
    grid = grid[jax.random.permutation(jax.random.fold_in(own, 1), rows)]
    turn = jax.random.randint(jax.random.fold_in(own, 2), (rows, 1), 0, top)
    return jnp.take_along_axis(grid, (jnp.arange(top)[None, :] + turn) % top, axis=1)


def load_shares(count, total, reach, lean, full):
    portions = [(1 << 20) // math.isqrt(grade ** lean) + 1 for grade in range(1, count + 1)]
    largest = reach if full else min(reach, max(-(-total // count), total * portions[0] // sum(portions)))
    least = 1 if total - largest >= count - 1 else 0
    given, surplus = [largest] + [least] * (count - 1), total - largest - least * (count - 1)
    while surplus > 0:
        free = [i for i in range(1, count) if given[i] < largest] or [i for i in range(1, count) if given[i] < reach]
        pool, left = sum([portions[i] for i in free]), surplus
        for i in free:
            more = min(reach - given[i], max(1, left * portions[i] // pool), surplus)
            given[i] = given[i] + more
            surplus = surplus - more
    return np.array(given)


def bell_draw(own_key, shape, spread, limit, split=(), kind=jnp.bfloat16):
    factor_of = block_scale(own_key, shape, split, -0.22, 0.18) if split else 1.0
    values = jax.random.normal(own_key, shape, jnp.float32) * spread * factor_of
    return jnp.minimum(jnp.maximum(values, -limit), limit).astype(kind)


def setup_inputs(seed: int = 0, part: int = 0) -> dict:
    keys = jax.random.split(jax.random.key(seed), 18)
    part_keys = jax.random.split(jax.random.fold_in(keys[17], part), 18)
    grid_latent = bell_draw(part_keys[0], (GRID, D), 1.0, 6.0, ((0, 16),))
    grid_band_keys = jax.random.split(jax.random.fold_in(part_keys[1], 1), GRID // GRID_DEV)
    grid_band_turns = jax.random.permutation(jax.random.fold_in(part_keys[1], 3), GRID // GRID_DEV)
    grid_band = jax.vmap(lambda own, number: assign_block(jax.random.fold_in(part_keys[1], 2), own, number, GRID_DEV, N_LAT, 1, CAP, 2))(grid_band_keys, grid_band_turns).reshape((GRID, 1))
    edge_rows = plant(jax.random.randint(part_keys[2], (GRID, KG), 0, MESH_PART), jax.random.fold_in(part_keys[2], 1), 0, MESH_PART - 1).astype(jnp.int32)
    mesh_latent = bell_draw(part_keys[3], (MESH, D), 1.0, 6.0, ((0, 8),))
    mesh_slots = draw_mesh_slots(jax.random.fold_in(jax.random.fold_in(keys[17], part), 71), part)
    send_rows = plant(jax.random.randint(part_keys[5], (NPART, 8, BND), 0, MESH_PART), jax.random.fold_in(part_keys[5], 1), 0, MESH_PART - 1).astype(jnp.int32)
    enc_send = bell_draw(keys[6], (D, D), D ** -0.5, 0.25)
    enc_recv = bell_draw(keys[7], (D, D), D ** -0.5, 0.25)
    enc_edge = bell_draw(keys[8], (D, D), D ** -0.5, 0.25)
    bias_grid = bell_draw(keys[9], (D,), 1.0, 4.0, (), jnp.float32)
    node_gain = jnp.clip(1.0 + 0.18 * jax.random.normal(keys[10], (D,), jnp.float32), 0.1, 1.9)
    proc_send = bell_draw(keys[11], (D, D), D ** -0.5, 0.25)
    proc_recv = bell_draw(keys[12], (D, D), D ** -0.5, 0.25)
    proc_edge = bell_draw(keys[13], (D, D), D ** -0.5, 0.25)
    bias_mesh = bell_draw(keys[14], (D,), 1.0, 4.0, (), jnp.float32)
    mesh_gain = jnp.clip(1.0 + 0.18 * jax.random.normal(keys[15], (D,), jnp.float32), 0.1, 1.9)
    cotangent = bell_draw(part_keys[16], (MESH, D), 1.0, 6.0, ((0, 8),))
    return dict(grid_latent=grid_latent, grid_band=grid_band, edge_rows=edge_rows, mesh_latent=mesh_latent, mesh_slots=mesh_slots, send_rows=send_rows, enc_send=enc_send, enc_recv=enc_recv, enc_edge=enc_edge, bias_grid=bias_grid, node_gain=node_gain, proc_send=proc_send, proc_recv=proc_recv, proc_edge=proc_edge, bias_mesh=bias_mesh, mesh_gain=mesh_gain, cotangent=cotangent)


EPS = 1e-05
LAT_STEPS = (-1, -1, -1, 0, 0, 1, 1, 1)
LON_STEPS = (-1, 0, 1, -1, 1, -1, 0, 1)

def layer_norm(value):
    centred = value - lax.optimization_barrier(jnp.mean(value, -1, keepdims=True))
    return centred * lax.rsqrt(lax.optimization_barrier(jnp.mean(centred * centred, -1, keepdims=True)) + EPS)

def norm_back(value, upstream):
    centred = value - lax.optimization_barrier(jnp.mean(value, -1, keepdims=True))
    inverse = lax.rsqrt(lax.optimization_barrier(jnp.mean(centred * centred, -1, keepdims=True)) + EPS)
    normed = centred * inverse
    inner = lax.optimization_barrier(jnp.mean(upstream * normed, -1, keepdims=True))
    return (upstream - lax.optimization_barrier(jnp.mean(upstream, -1, keepdims=True)) - normed * inner) * inverse

def silu_slope(value):
    sigma = jax.nn.sigmoid(value)
    return sigma * (1.0 + value * (1.0 - sigma))

def dot_plain(left, right):
    return jnp.dot(left, right, preferred_element_type=jnp.float32)

def dot_trans(left, right):
    return lax.dot_general(left, right, (((1,), (1,)), ((), ())), preferred_element_type=jnp.float32)

def reference(grid_latent, grid_band, edge_rows, mesh_latent, mesh_slots, send_rows, enc_send, enc_recv, enc_edge, bias_grid, node_gain, proc_send, proc_recv, proc_edge, bias_mesh, mesh_gain, cotangent):
    grid_index = jnp.arange(GRID, dtype=jnp.int32)
    grid_part = grid_index // (GRID_DEV * N_SUB)
    grid_sector = grid_part % N_LON
    target = ((grid_band[:, 0] * N_LON + grid_sector) * MESH_PART)[:, None] + edge_rows
    mesh_index = jnp.arange(MESH, dtype=jnp.int32)
    own_part = mesh_index // MESH_PART
    own_band = own_part // N_LON
    own_sector = own_part % N_LON
    is_halo = mesh_slots >= MESH_PART
    offset = jnp.maximum(mesh_slots - MESH_PART, 0)
    direction = offset // BND
    within = offset % BND
    lat_move = jnp.array(LAT_STEPS, dtype=jnp.int32)[direction]
    lon_move = jnp.array(LON_STEPS, dtype=jnp.int32)[direction]
    src_band = jnp.clip(own_band[:, None] - lat_move, 0, N_LAT - 1)
    src_sector = (own_sector[:, None] - lon_move) % N_LON
    src_part = (src_band * N_LON + src_sector).astype(jnp.int32)
    halo_row = send_rows[src_part, direction, within]
    sender = jnp.where(is_halo, src_part * MESH_PART + halo_row, own_part[:, None] * MESH_PART + mesh_slots).astype(jnp.int32)
    proj_grid = dot_plain(grid_latent, enc_send).astype(jnp.bfloat16)
    proj_mesh = dot_plain(mesh_latent, enc_recv).astype(jnp.bfloat16)

    def grid_edge(k):
        pre_grid = proj_grid.astype(jnp.float32) + proj_mesh[target[:, k]].astype(jnp.float32) + bias_grid
        hid_grid = jax.nn.silu(pre_grid).astype(jnp.bfloat16)
        return (pre_grid, dot_plain(hid_grid, enc_edge))
    agg_grid = jnp.zeros((MESH, D), jnp.float32)
    for k in range(KG):
        pre_grid, z_grid = grid_edge(k)
        agg_grid = agg_grid + jax.ops.segment_sum(layer_norm(z_grid), target[:, k], num_segments=MESH)
    mesh_mid = (mesh_latent.astype(jnp.float32) + layer_norm(agg_grid) * node_gain).astype(jnp.bfloat16)
    send_mesh = dot_plain(mesh_mid, proc_send).astype(jnp.bfloat16)
    recv_mesh = dot_plain(mesh_mid, proc_recv).astype(jnp.bfloat16)

    def mesh_edge(k):
        pre_mesh = send_mesh[sender[:, k]].astype(jnp.float32) + recv_mesh.astype(jnp.float32) + bias_mesh
        hid_mesh = jax.nn.silu(pre_mesh).astype(jnp.bfloat16)
        return (pre_mesh, dot_plain(hid_mesh, proc_edge))
    agg_mesh = jnp.zeros((MESH, D), jnp.float32)
    for k in range(KM):
        pre_mesh, z_mesh = mesh_edge(k)
        agg_mesh = agg_mesh + layer_norm(z_mesh)
    mesh_out = (mesh_mid.astype(jnp.float32) + layer_norm(agg_mesh) * mesh_gain).astype(jnp.bfloat16)
    upstream = cotangent.astype(jnp.float32)
    d_agg_mesh = norm_back(agg_mesh, upstream * mesh_gain)
    d_send = jnp.zeros((MESH, D), jnp.float32)
    d_recv = jnp.zeros((MESH, D), jnp.float32)
    for k in range(KM):
        pre_mesh, z_mesh = mesh_edge(k)
        d_z_mesh = norm_back(z_mesh, d_agg_mesh).astype(jnp.bfloat16)
        d_pre_mesh = (dot_trans(d_z_mesh, proc_edge) * silu_slope(pre_mesh)).astype(jnp.bfloat16).astype(jnp.float32)
        d_recv = d_recv + d_pre_mesh
        d_send = d_send + jax.ops.segment_sum(d_pre_mesh, sender[:, k], num_segments=MESH)
    d_mid = upstream + dot_trans(d_send.astype(jnp.bfloat16), proc_send) + dot_trans(d_recv.astype(jnp.bfloat16), proc_recv)
    d_agg_grid = norm_back(agg_grid, d_mid * node_gain)
    d_proj_grid = jnp.zeros((GRID, D), jnp.float32)
    d_proj_mesh = jnp.zeros((MESH, D), jnp.float32)
    for k in range(KG):
        pre_grid, z_grid = grid_edge(k)
        d_z_grid = norm_back(z_grid, d_agg_grid[target[:, k]]).astype(jnp.bfloat16)
        d_pre_grid = (dot_trans(d_z_grid, enc_edge) * silu_slope(pre_grid)).astype(jnp.bfloat16).astype(jnp.float32)
        d_proj_grid = d_proj_grid + d_pre_grid
        d_proj_mesh = d_proj_mesh + jax.ops.segment_sum(d_pre_grid, target[:, k], num_segments=MESH)
    grid_grad = dot_trans(d_proj_grid.astype(jnp.bfloat16), enc_send).astype(jnp.bfloat16)
    mesh_grad = (d_mid + dot_trans(d_proj_mesh.astype(jnp.bfloat16), enc_recv)).astype(jnp.bfloat16)
    return (mesh_out, mesh_grad, grid_grad)
```

```python
import functools

import jax
import jax.numpy as jnp
from jax import lax
from jax.experimental import pallas as pl
from jax.experimental.pallas import tpu as pltpu
from jax.sharding import PartitionSpec as P

EPS = 1e-05
DIRECTIONS = ((-1, -1), (-1, 0), (-1, 1), (0, -1), (0, 1), (1, -1), (1, 0), (1, 1))
MESH = pl.DeviceIdType.MESH
F32 = jnp.float32
BF16 = jnp.bfloat16
CHUNK = 64


def dot_plain(left, right):
    return jnp.dot(left, right, preferred_element_type=F32)


def dot_trans(left, right):
    return lax.dot_general(left, right, (((1,), (1,)), ((), ())), preferred_element_type=F32)


def row_mean(value):
    return jnp.mean(value, -1, keepdims=True)


def norm_parts(value):
    centred = value - row_mean(value)
    inverse = lax.rsqrt(row_mean(centred * centred) + EPS)
    return centred * inverse, inverse


def norm_back(normed, inverse, upstream):
    inner = row_mean(upstream * normed)
    return (upstream - row_mean(upstream) - normed * inner) * inverse


def silu_slope(value):
    sigma = jax.nn.sigmoid(value)
    return sigma * (1.0 + value * (1.0 - sigma))


def iota_f32(shape, axis):
    return lax.broadcasted_iota(jnp.int32, shape, axis).astype(F32)


def as_row(column):
    n = column.shape[0]
    shape = (n, n)
    same = lax.broadcasted_iota(jnp.int32, shape, 0) == lax.broadcasted_iota(jnp.int32, shape, 1)
    return jnp.sum(jnp.where(same, column, 0.0), 0, keepdims=True)


def hot_rows(column, count):
    return (column == iota_f32((column.shape[0], count), 1)).astype(F32).astype(BF16)


def hot_columns(row, count):
    return (row == iota_f32((count, row.shape[1]), 0)).astype(F32).astype(BF16)


def kernel(
    bands,
    sectors,
    grid_ref,
    band_ref,
    rows_ref,
    mesh_ref,
    slots_ref,
    send_ref,
    enc_send_hbm,
    enc_recv_hbm,
    enc_edge_hbm,
    bias_grid_ref,
    node_gain_ref,
    proc_send_hbm,
    proc_recv_hbm,
    proc_edge_hbm,
    bias_mesh_ref,
    mesh_gain_ref,
    cot_ref,
    mesh_out_ref,
    mesh_grad_ref,
    grid_grad_ref,
    enc_send,
    enc_recv,
    enc_edge,
    proc_send,
    proc_recv,
    proc_edge,
    slots_mine,
    slots_peer,
    gathered_mesh,
    proj_grid,
    pre_grid,
    z_grid,
    inv_grid,
    hid,
    work,
    part_mine,
    part_out,
    part_in,
    lat_out,
    lat_in,
    mid_full,
    bound_out,
    table,
    pre_mesh,
    z_mesh,
    out_half_peer,
    out_half_mine,
    back_out,
    back_in,
    send_part_out,
    send_part_in,
    d_agg_all,
    part_out_2,
    part_in_2,
    lat_out_2,
    lat_in_2,
    grad_half_mine,
    grad_half_peer,
    w_sem,
    lat_s,
    lat_r,
    fwd_s,
    fwd_r,
    sub_s,
    sub_r,
    nb_s,
    nb_r,
):
    lat, lon, sub = lax.axis_index("lat"), lax.axis_index("lon"), lax.axis_index("sub")
    other = 1 - sub
    nodes, width = grid_ref.shape
    fanout = rows_ref.shape[1]
    mesh_rows = mesh_ref.shape[0]
    half = mesh_rows // 2
    half_all = bands * half
    bound = send_ref.shape[2]
    edges_half = 2 * slots_ref.shape[1]
    table_rows = table.shape[0]

    weights = (
        (enc_send_hbm, enc_send),
        (enc_recv_hbm, enc_recv),
        (enc_edge_hbm, enc_edge),
        (proc_send_hbm, proc_send),
        (proc_recv_hbm, proc_recv),
        (proc_edge_hbm, proc_edge),
    )
    loads = [pltpu.make_async_copy(a, b, w_sem.at[n]) for n, (a, b) in enumerate(weights)]
    for load in loads:
        load.start()

    slots_mine[...] = jnp.zeros_like(slots_mine)
    slots_mine[:, 0 : slots_ref.shape[1]] = slots_ref[...]
    table[mesh_rows:, :] = jnp.zeros((table_rows - mesh_rows, width), BF16)
    back_in[...] = jnp.zeros_like(back_in)

    barrier = pltpu.get_barrier_semaphore()

    def lat_peer(step):
        return lax.rem(lat + step, bands)

    def reaches(d):
        target = lat + DIRECTIONS[d][0]
        return (target >= 0) & (target < bands)

    def comes_from(d):
        target = lat - DIRECTIONS[d][0]
        return (target >= 0) & (target < bands)

    def neighbour(d, sign):
        return {
            "lat": lat + sign * DIRECTIONS[d][0],
            "lon": lax.rem(lon + sign * DIRECTIONS[d][1] + sectors, sectors),
        }

    for step in range(1, bands):
        pl.semaphore_signal(barrier, inc=1, device_id={"lat": lat_peer(step)}, device_id_type=MESH)
    pl.semaphore_signal(barrier, inc=1, device_id={"sub": other}, device_id_type=MESH)
    diagonal = [d for d in range(8) if DIRECTIONS[d][1] != 0]
    for d in diagonal:
        @pl.when(reaches(d))
        def _():
            pl.semaphore_signal(barrier, inc=1, device_id=neighbour(d, 1), device_id_type=MESH)
    near = 2 + 2 * (lat > 0).astype(jnp.int32) + 2 * (lat < bands - 1).astype(jnp.int32)
    pl.semaphore_wait(barrier, bands + near)

    def half_rows(which, band):
        return pl.ds(pl.multiple_of(which * half_all + band * half, half), half)

    def band_rows(band):
        return pl.ds(pl.multiple_of(band * half, half), half)

    my_rows = pl.ds(pl.multiple_of(sub * half, half), half)
    peer_rows = pl.ds(pl.multiple_of(other * half, half), half)

    def to_sub(source, target, n):
        return pltpu.make_async_remote_copy(
            src_ref=source,
            dst_ref=target,
            send_sem=sub_s.at[n],
            recv_sem=sub_r.at[n],
            device_id={"sub": other},
            device_id_type=MESH,
        )

    def to_lat(source, target, n, step):
        return pltpu.make_async_remote_copy(
            src_ref=source,
            dst_ref=target,
            send_sem=lat_s.at[n, step],
            recv_sem=lat_r.at[n, step],
            device_id={"lat": lat_peer(step)},
            device_id_type=MESH,
        )

    def gather_start(source, whole, n):
        copies = []
        for step in range(1, bands):
            copy = to_lat(source, whole.at[half_rows(sub, lat)], n, step)
            copy.start()
            copies.append(copy)
        return copies

    def gather_finish(copies, whole, n):
        onward = []
        for step in range(1, bands):
            copies[step - 1].wait_recv()
            origin = lax.rem(lat - step + bands, bands)
            copy = pltpu.make_async_remote_copy(
                src_ref=whole.at[half_rows(sub, origin)],
                dst_ref=whole.at[half_rows(sub, origin)],
                send_sem=fwd_s.at[n, step],
                recv_sem=fwd_r.at[n, step],
                device_id={"sub": other},
                device_id_type=MESH,
            )
            copy.start()
            onward.append(copy)
        for copy in onward:
            copy.wait_recv()
        return onward

    slot_copy = to_sub(slots_mine.at[peer_rows], slots_peer, 0)
    slot_copy.start()
    gather_1 = gather_start(mesh_ref.at[my_rows], gathered_mesh, 0)
    gathered_mesh[half_rows(0, lat), :] = mesh_ref[0:half, :]
    gathered_mesh[half_rows(1, lat), :] = mesh_ref[half:, :]

    bias_grid = bias_grid_ref[...].reshape(1, width)
    bias_mesh = bias_mesh_ref[...].reshape(1, width)
    node_gain = node_gain_ref[...].reshape(1, width)
    mesh_gain = mesh_gain_ref[...].reshape(1, width)

    loads[0].wait()
    proj_grid[...] = dot_plain(grid_ref[...], enc_send[...]).astype(BF16)

    band_of = band_ref[...]
    hots, hots_t = [], []
    for k in range(fanout):
        row = rows_ref[:, k : k + 1]
        upper = (row >= half).astype(jnp.int32)
        place = (upper * (half_all - half) + band_of * half + row).astype(F32)
        hots.append(hot_rows(place, 2 * half_all))
        hots_t.append(hot_columns(as_row(place), 2 * half_all))
    hot_t = jnp.concatenate(hots_t, 1)

    listed = jnp.concatenate(
        [jnp.broadcast_to(send_ref[0, d : d + 1, :], (bound, bound)) for d in range(8)], 0
    ).astype(F32)
    lane = lax.broadcasted_iota(jnp.int32, (8 * bound, bound), 1)
    line = lax.rem(lax.broadcasted_iota(jnp.int32, (8 * bound, bound), 0), bound)
    list_column = jnp.sum(jnp.where(lane == line, listed, 0.0), 1, keepdims=True)
    pick = hot_rows(list_column, mesh_rows)
    pick_t = hot_columns(as_row(list_column), mesh_rows)

    slot_copy.wait()
    own_slots = slots_ref[my_rows, :].astype(F32)
    their_slots = slots_peer[...].astype(F32)
    slot_column = jnp.concatenate(
        [own_slots[:, k : k + 1] for k in range(edges_half // 2)]
        + [their_slots[:, k : k + 1] for k in range(edges_half // 2)],
        0,
    )
    slot_hot = hot_rows(slot_column, table_rows)
    slot_hot_t = hot_columns(as_row(slot_column), table_rows)

    loads[1].wait()
    loads[2].wait()
    onward_1 = gather_finish(gather_1, gathered_mesh, 0)
    proj_mesh = dot_plain(gathered_mesh[...], enc_recv[...]).astype(BF16)
    for k in range(fanout):
        base = k * nodes
        pre_grid[base : base + nodes, :] = dot_plain(hots[k], proj_mesh)
        for at in range(0, nodes, CHUNK):
            here = slice(base + at, base + at + CHUNK)
            pre = pre_grid[here, :] + proj_grid[at : at + CHUNK, :].astype(F32) + bias_grid
            pre_grid[here, :] = pre
            hid[here, :] = (pre * jax.nn.sigmoid(pre)).astype(BF16)
        z_grid[base : base + nodes, :] = dot_plain(hid[base : base + nodes, :], enc_edge[...])
        for at in range(base, base + nodes, CHUNK):
            here = slice(at, at + CHUNK)
            normed, inverse = norm_parts(z_grid[here, :])
            z_grid[here, :] = normed
            inv_grid[here, :] = inverse
            hid[here, :] = normed.astype(BF16)

    def scatter_sum(values, mine, out, inbound, out_lat, in_lat, n_sub, n_lat, meanwhile):
        total = dot_plain(hot_t, values)
        low, high = total[0:half_all, :], total[half_all:, :]
        out[...] = jnp.where(sub == 0, high, low).astype(BF16)
        copy = to_sub(out, inbound, n_sub)
        copy.start()
        mine[...] = jnp.where(sub == 0, low, high)
        meanwhile()
        copy.wait()
        copies = []
        for step in range(bands - 1, 0, -1):
            rows = band_rows(lat_peer(step))
            out_lat[rows, :] = (mine[rows, :] + inbound[rows, :].astype(F32)).astype(BF16)
            copy = to_lat(out_lat.at[rows], in_lat.at[step], n_lat, step)
            copy.start()
            copies.append(copy)
        rows = band_rows(lat)
        own = mine[rows, :] + inbound[rows, :].astype(F32)
        return own, copies

    def scatter_finish(own, copies, in_lat):
        for copy in copies:
            copy.wait()
        for step in range(1, bands):
            own = own + in_lat[step].astype(F32)
        return own

    def slope_of(ref, start, stop):
        for at in range(start, stop, CHUNK):
            ref[at : at + CHUNK, :] = silu_slope(ref[at : at + CHUNK, :])

    own, copies = scatter_sum(
        hid[...], part_mine, part_out, part_in, lat_out, lat_in, 1, 1, lambda: None
    )
    slope_of(pre_grid, 0, fanout * nodes)
    for n in range(3, 6):
        loads[n].wait()
    agg_grid = scatter_finish(own, copies, lat_in)

    agg_grid_normed, agg_grid_inverse = norm_parts(agg_grid)
    mid_half = (mesh_ref[my_rows, :].astype(F32) + agg_grid_normed * node_gain).astype(BF16)
    mid_full[my_rows, :] = mid_half
    mid_copy = to_sub(mid_full.at[my_rows], mid_full.at[my_rows], 2)
    mid_copy.start()
    recv_half = dot_plain(mid_half, proc_recv[...]).astype(BF16).astype(F32) + bias_mesh
    mid_copy.wait()
    send_mesh = dot_plain(mid_full[...], proc_send[...]).astype(BF16)
    bound_out[...] = dot_plain(pick, send_mesh).astype(BF16)

    def block_of(d):
        return pl.ds(d * bound, bound)

    def table_of(d):
        return pl.ds(mesh_rows + d * bound, bound)

    def to_near(source, target, n, d, sign):
        return pltpu.make_async_remote_copy(
            src_ref=source,
            dst_ref=target,
            send_sem=nb_s.at[n, d],
            recv_sem=nb_r.at[n, d],
            device_id=neighbour(d, sign),
            device_id_type=MESH,
        )

    for d in range(8):
        @pl.when(reaches(d))
        def _():
            to_near(bound_out.at[block_of(d)], table.at[table_of(d)], 0, d, 1).start()
    table[0:mesh_rows, :] = send_mesh
    for d in range(8):
        copy = to_near(bound_out.at[block_of(d)], table.at[table_of(d)], 0, d, 1)

        @pl.when(comes_from(d))
        def _():
            copy.wait_recv()

    edges = edges_half * half
    pre_mesh[...] = dot_plain(slot_hot, table[...])
    for at in range(0, edges, half):
        here = slice(at, at + half)
        pre = pre_mesh[here, :] + recv_half
        pre_mesh[here, :] = pre
        hid[here, :] = (pre * jax.nn.sigmoid(pre)).astype(BF16)
    z_mesh[...] = dot_plain(hid[0:edges, :], proc_edge[...])
    agg_mesh = jnp.zeros((half, width), F32)
    inverses = []
    for at in range(0, edges, half):
        here = slice(at, at + half)
        normed, inverse = norm_parts(z_mesh[here, :])
        z_mesh[here, :] = normed
        inverses.append(inverse)
        agg_mesh = agg_mesh + normed

    agg_mesh_normed, agg_mesh_inverse = norm_parts(agg_mesh)
    out_half = (mid_half.astype(F32) + agg_mesh_normed * mesh_gain).astype(BF16)
    out_half_mine[...] = out_half
    mesh_out_ref[my_rows, :] = out_half
    out_copy = to_sub(out_half_mine, out_half_peer, 3)
    out_copy.start()

    upstream = cot_ref[my_rows, :].astype(F32)
    d_agg_mesh = norm_back(agg_mesh_normed, agg_mesh_inverse, upstream * mesh_gain)
    for n, at in enumerate(range(0, edges, half)):
        here = slice(at, at + half)
        hid[here, :] = norm_back(z_mesh[here, :], inverses[n], d_agg_mesh).astype(BF16)
    work[0:edges, :] = dot_trans(hid[0:edges, :], proc_edge[...])
    d_recv = jnp.zeros((half, width), F32)
    for at in range(0, edges, half):
        here = slice(at, at + half)
        d_pre = (work[here, :] * silu_slope(pre_mesh[here, :])).astype(BF16)
        hid[here, :] = d_pre
        d_recv = d_recv + d_pre.astype(F32)
    d_table = dot_plain(slot_hot_t, hid[0:edges, :])
    back_out[...] = d_table[mesh_rows : mesh_rows + 8 * bound, :].astype(BF16)
    for d in range(8):
        @pl.when(comes_from(d))
        def _():
            to_near(back_out.at[block_of(d)], back_in.at[block_of(d)], 1, d, -1).start()
    d_mid = upstream + dot_trans(d_recv.astype(BF16), proc_recv[...])
    for d in range(8):
        copy = to_near(back_out.at[block_of(d)], back_in.at[block_of(d)], 1, d, -1)

        @pl.when(reaches(d))
        def _():
            copy.wait_recv()
    d_send = d_table[0:mesh_rows, :] + dot_plain(pick_t, back_in[...])
    send_part_out[...] = jnp.where(sub == 0, d_send[half:, :], d_send[0:half, :])
    send_copy = to_sub(send_part_out, send_part_in, 4)
    send_copy.start()
    d_send_half = jnp.where(sub == 0, d_send[0:half, :], d_send[half:, :])
    send_copy.wait()
    d_send_half = d_send_half + send_part_in[...]
    d_mid = d_mid + dot_trans(d_send_half.astype(BF16), proc_send[...])
    d_agg_grid = norm_back(agg_grid_normed, agg_grid_inverse, d_mid * node_gain)
    d_agg_all[half_rows(sub, lat), :] = d_agg_grid.astype(BF16)
    own_copy = to_sub(d_agg_all.at[half_rows(sub, lat)], d_agg_all.at[half_rows(sub, lat)], 5)
    own_copy.start()
    gather_2 = gather_start(d_agg_all.at[half_rows(sub, lat)], d_agg_all, 2)
    out_copy.wait()
    mesh_out_ref[peer_rows, :] = out_half_peer[...]
    onward_2 = gather_finish(gather_2, d_agg_all, 1)
    own_copy.wait()

    for k in range(fanout):
        base = k * nodes
        work[base : base + nodes, :] = dot_plain(hots[k], d_agg_all[...])
        for at in range(base, base + nodes, CHUNK):
            here = slice(at, at + CHUNK)
            hid[here, :] = norm_back(z_grid[here, :], inv_grid[here, :], work[here, :]).astype(BF16)
        work[base : base + nodes, :] = dot_trans(hid[base : base + nodes, :], enc_edge[...])
        for at in range(base, base + nodes, CHUNK):
            here = slice(at, at + CHUNK)
            hid[here, :] = (work[here, :] * pre_grid[here, :]).astype(BF16)

    def grid_side():
        total = hid[0:nodes, :].astype(F32)
        for k in range(1, fanout):
            total = total + hid[k * nodes : (k + 1) * nodes, :].astype(F32)
        grid_grad_ref[...] = dot_trans(total.astype(BF16), enc_send[...]).astype(BF16)

    own, copies_2 = scatter_sum(
        hid[...], part_mine, part_out_2, part_in_2, lat_out_2, lat_in_2, 6, 3, lambda: None
    )
    grid_side()
    d_proj_mesh = scatter_finish(own, copies_2, lat_in_2)
    grad_half = (d_mid + dot_trans(d_proj_mesh.astype(BF16), enc_recv[...])).astype(BF16)
    grad_half_mine[...] = grad_half
    grad_copy = to_sub(grad_half_mine, grad_half_peer, 7)
    grad_copy.start()
    mesh_grad_ref[my_rows, :] = grad_half
    for copy in gather_1 + gather_2 + onward_1 + onward_2:
        copy.wait_send()
    for d in range(8):
        @pl.when(reaches(d))
        def _():
            to_near(bound_out.at[block_of(d)], table.at[table_of(d)], 0, d, 1).wait_send()

        @pl.when(comes_from(d))
        def _():
            to_near(back_out.at[block_of(d)], back_in.at[block_of(d)], 1, d, -1).wait_send()
    grad_copy.wait()
    mesh_grad_ref[peer_rows, :] = grad_half_peer[...]


def on_device(bands, sectors, *args):
    grid_latent, mesh_latent, mesh_slots = args[0], args[3], args[4]
    send_rows, edge_rows = args[5], args[2]
    nodes, width = grid_latent.shape
    mesh_rows = mesh_latent.shape[0]
    half = mesh_rows // 2
    bound = 8 * send_rows.shape[2]
    table_rows = -(-(mesh_rows + bound) // 128) * 128
    edges = edge_rows.shape[1] * nodes
    mesh_edges = 2 * mesh_slots.shape[1] * half
    every = bands * mesh_rows
    most = max(edges, mesh_edges)
    vmem = pl.BlockSpec(memory_space=pltpu.VMEM)
    hbm = pl.BlockSpec(memory_space=pl.ANY)
    weights = (6, 7, 8, 11, 12, 13)
    dma = pltpu.SemaphoreType.DMA
    return pl.pallas_call(
        functools.partial(kernel, bands, sectors),
        out_shape=(
            jax.ShapeDtypeStruct((mesh_rows, width), BF16),
            jax.ShapeDtypeStruct((mesh_rows, width), BF16),
            jax.ShapeDtypeStruct((nodes, width), BF16),
        ),
        in_specs=[hbm if n in weights else vmem for n in range(len(args))],
        out_specs=(vmem, vmem, vmem),
        scratch_shapes=[pltpu.VMEM((width, width), BF16)] * 6
        + [
            pltpu.VMEM((mesh_rows, 128), jnp.int32),
            pltpu.VMEM((half, 128), jnp.int32),
            pltpu.VMEM((every, width), BF16),
            pltpu.VMEM((nodes, width), BF16),
            pltpu.VMEM((edges, width), F32),
            pltpu.VMEM((edges, width), F32),
            pltpu.VMEM((edges, 1), F32),
            pltpu.VMEM((most, width), BF16),
            pltpu.VMEM((most, width), F32),
            pltpu.VMEM((every // 2, width), F32),
            pltpu.VMEM((every // 2, width), BF16),
            pltpu.VMEM((every // 2, width), BF16),
            pltpu.VMEM((every // 2, width), BF16),
            pltpu.VMEM((bands, half, width), BF16),
            pltpu.VMEM((mesh_rows, width), BF16),
            pltpu.VMEM((bound, width), BF16),
            pltpu.VMEM((table_rows, width), BF16),
            pltpu.VMEM((mesh_edges, width), F32),
            pltpu.VMEM((mesh_edges, width), F32),
            pltpu.VMEM((half, width), BF16),
            pltpu.VMEM((half, width), BF16),
            pltpu.VMEM((bound, width), BF16),
            pltpu.VMEM((bound, width), BF16),
            pltpu.VMEM((half, width), F32),
            pltpu.VMEM((half, width), F32),
            pltpu.VMEM((every, width), BF16),
            pltpu.VMEM((every // 2, width), BF16),
            pltpu.VMEM((every // 2, width), BF16),
            pltpu.VMEM((every // 2, width), BF16),
            pltpu.VMEM((bands, half, width), BF16),
            pltpu.VMEM((half, width), BF16),
            pltpu.VMEM((half, width), BF16),
            dma((6,)),
            dma((4, bands)),
            dma((4, bands)),
            dma((2, bands)),
            dma((2, bands)),
            dma((8,)),
            dma((8,)),
            dma((2, 8)),
            dma((2, 8)),
        ],
        compiler_params=pltpu.CompilerParams(
            collective_id=0, has_side_effects=True, vmem_limit_bytes=48 * 1024 * 1024
        ),
    )(*args)


def solution(mesh):
    part = P(("group", "lat", "lon"), None)
    node = P(("group", "lat", "lon", "sub"), None)
    placed = (
        (node, node, node, part, P(("group", "lat", "lon"), "sub"))
        + (P(("group", "lat", "lon"), None, None),)
        + (P(),) * 10
        + (part,)
    )
    return jax.shard_map(
        functools.partial(on_device, mesh.shape["lat"], mesh.shape["lon"]),
        mesh=mesh,
        in_specs=placed,
        out_specs=(part, part, node),
        check_vma=False,
    )
```

```python
import functools

import jax
import jax.numpy as jnp
from jax import lax
from jax.experimental import pallas as pl
from jax.experimental.pallas import tpu as pltpu
from jax.sharding import PartitionSpec as P

EPS = 1e-05
DIRECTIONS = ((-1, -1), (-1, 0), (-1, 1), (0, -1), (0, 1), (1, -1), (1, 0), (1, 1))
MESH = pl.DeviceIdType.MESH
F32 = jnp.float32
BF16 = jnp.bfloat16
CHUNK = 64


def dot_plain(left, right):
    return jnp.dot(left, right, preferred_element_type=F32)


def dot_trans(left, right):
    return lax.dot_general(left, right, (((1,), (1,)), ((), ())), preferred_element_type=F32)


def row_mean(value):
    return jnp.mean(value, -1, keepdims=True)


def norm_parts(value):
    centred = value - row_mean(value)
    inverse = lax.rsqrt(row_mean(centred * centred) + EPS)
    return centred * inverse, inverse


def norm_back(normed, inverse, upstream):
    inner = row_mean(upstream * normed)
    return (upstream - row_mean(upstream) - normed * inner) * inverse


def silu_slope(value):
    sigma = jax.nn.sigmoid(value)
    return sigma * (1.0 + value * (1.0 - sigma))


def iota_f32(shape, axis):
    return lax.broadcasted_iota(jnp.int32, shape, axis).astype(F32)


def as_row(column):
    n = column.shape[0]
    shape = (n, n)
    same = lax.broadcasted_iota(jnp.int32, shape, 0) == lax.broadcasted_iota(jnp.int32, shape, 1)
    return jnp.sum(jnp.where(same, column, 0.0), 0, keepdims=True)


def as_column(row):
    n = row.shape[1]
    shape = (n, n)
    same = lax.broadcasted_iota(jnp.int32, shape, 0) == lax.broadcasted_iota(jnp.int32, shape, 1)
    return jnp.sum(jnp.where(same, row, 0.0), 1, keepdims=True)


def hot_rows(column, count):
    return (column == iota_f32((column.shape[0], count), 1)).astype(F32).astype(BF16)


def hot_columns(row, count):
    return (row == iota_f32((count, row.shape[1]), 0)).astype(F32).astype(BF16)


def kernel(
    bands,
    sectors,
    *refs,
):
    inputs, outputs, local = refs[:17], refs[17:20], refs[20:37]
    body(bands, sectors, inputs, *local, *outputs, *refs[37:])


def body(
    bands,
    sectors,
    inputs,
    grid_ref,
    band_ref,
    rows_ref,
    mesh_ref,
    slots_ref,
    send_ref,
    enc_send,
    enc_recv,
    enc_edge,
    bias_grid_ref,
    node_gain_ref,
    proc_send,
    proc_recv,
    proc_edge,
    bias_mesh_ref,
    mesh_gain_ref,
    cot_ref,
    mesh_out_ref,
    mesh_grad_ref,
    grid_grad_ref,
    slots_mine,
    slots_peer,
    gathered_mesh,
    proj_grid,
    pre_grid,
    z_grid,
    inv_grid,
    hid,
    work,
    part_mine,
    part_out,
    part_in,
    lat_out,
    lat_in,
    mid_full,
    bound_out,
    table,
    pre_mesh,
    z_mesh,
    out_half_peer,
    out_half_mine,
    back_out,
    back_in,
    send_part_out,
    send_part_in,
    d_agg_all,
    part_out_2,
    part_in_2,
    lat_out_2,
    lat_in_2,
    grad_half_mine,
    grad_half_peer,
    w_sem,
    lat_s,
    lat_r,
    fwd_s,
    fwd_r,
    sub_s,
    sub_r,
    nb_s,
    nb_r,
):
    lat, lon, sub = lax.axis_index("lat"), lax.axis_index("lon"), lax.axis_index("sub")
    other = 1 - sub
    nodes, width = grid_ref.shape
    fanout = rows_ref.shape[0]
    mesh_rows = mesh_ref.shape[0]
    half = mesh_rows // 2
    half_all = bands * half
    bound = send_ref.shape[2]
    own_slots = slots_ref.shape[0]
    edges_half = 2 * own_slots
    table_rows = table.shape[0]

    places = (
        grid_ref, band_ref, rows_ref, mesh_ref, slots_ref, send_ref, enc_send, enc_recv, enc_edge,
        bias_grid_ref, node_gain_ref, proc_send, proc_recv, proc_edge, bias_mesh_ref,
        mesh_gain_ref, cot_ref,
    )
    loads = [
        pltpu.make_async_copy(a, b, w_sem.at[n]) for n, (a, b) in enumerate(zip(inputs, places))
    ]
    early = (3, 4, 0, 6, 1, 2, 5)
    for n in early + tuple(n for n in range(17) if n not in early):
        loads[n].start()

    slots_mine[...] = jnp.zeros_like(slots_mine)
    table[mesh_rows:, :] = jnp.zeros((table_rows - mesh_rows, width), BF16)
    back_in[...] = jnp.zeros_like(back_in)

    barrier = pltpu.get_barrier_semaphore()

    def lat_peer(step):
        return lax.rem(lat + step, bands)

    def reaches(d):
        target = lat + DIRECTIONS[d][0]
        return (target >= 0) & (target < bands)

    def comes_from(d):
        target = lat - DIRECTIONS[d][0]
        return (target >= 0) & (target < bands)

    def neighbour(d, sign):
        return {
            "lat": lat + sign * DIRECTIONS[d][0],
            "lon": lax.rem(lon + sign * DIRECTIONS[d][1] + sectors, sectors),
        }

    for step in range(1, bands):
        pl.semaphore_signal(barrier, inc=1, device_id={"lat": lat_peer(step)}, device_id_type=MESH)
    pl.semaphore_signal(barrier, inc=1, device_id={"sub": other}, device_id_type=MESH)
    diagonal = [d for d in range(8) if DIRECTIONS[d][1] != 0]
    for d in diagonal:
        @pl.when(reaches(d))
        def _():
            pl.semaphore_signal(barrier, inc=1, device_id=neighbour(d, 1), device_id_type=MESH)
    near = 2 + 2 * (lat > 0).astype(jnp.int32) + 2 * (lat < bands - 1).astype(jnp.int32)
    loads[3].wait()
    loads[4].wait()
    slots_mine[0:own_slots, 0:mesh_rows] = slots_ref[...]
    pl.semaphore_wait(barrier, bands + near)

    def half_rows(which, band):
        return pl.ds(pl.multiple_of(which * half_all + band * half, half), half)

    def band_rows(band):
        return pl.ds(pl.multiple_of(band * half, half), half)

    my_rows = pl.ds(pl.multiple_of(sub * half, half), half)
    peer_rows = pl.ds(pl.multiple_of(other * half, half), half)

    def to_sub(source, target, n):
        return pltpu.make_async_remote_copy(
            src_ref=source,
            dst_ref=target,
            send_sem=sub_s.at[n],
            recv_sem=sub_r.at[n],
            device_id={"sub": other},
            device_id_type=MESH,
        )

    def to_lat(source, target, n, step):
        return pltpu.make_async_remote_copy(
            src_ref=source,
            dst_ref=target,
            send_sem=lat_s.at[n, step],
            recv_sem=lat_r.at[n, step],
            device_id={"lat": lat_peer(step)},
            device_id_type=MESH,
        )

    def gather_start(source, whole, n):
        copies = []
        for step in range(1, bands):
            copy = to_lat(source, whole.at[half_rows(sub, lat)], n, step)
            copy.start()
            copies.append(copy)
        return copies

    def gather_finish(copies, whole, n):
        onward = []
        for step in range(1, bands):
            copies[step - 1].wait_recv()
            origin = lax.rem(lat - step + bands, bands)
            copy = pltpu.make_async_remote_copy(
                src_ref=whole.at[half_rows(sub, origin)],
                dst_ref=whole.at[half_rows(sub, origin)],
                send_sem=fwd_s.at[n, step],
                recv_sem=fwd_r.at[n, step],
                device_id={"sub": other},
                device_id_type=MESH,
            )
            copy.start()
            onward.append(copy)
        for copy in onward:
            copy.wait_recv()
        return onward

    slot_copy = to_sub(slots_mine, slots_peer, 0)
    slot_copy.start()
    gather_1 = gather_start(mesh_ref.at[my_rows], gathered_mesh, 0)
    gathered_mesh[half_rows(0, lat), :] = mesh_ref[0:half, :]
    gathered_mesh[half_rows(1, lat), :] = mesh_ref[half:, :]

    for n in (0, 6, 9):
        loads[n].wait()
    bias_grid = bias_grid_ref[...].reshape(1, width)
    proj_grid[...] = (dot_plain(grid_ref[...], enc_send[...])).astype(BF16).astype(F32) + bias_grid

    for n in (1, 2, 5):
        loads[n].wait()
    band_of = band_ref[...]
    hots, hots_t = [], []
    for k in range(fanout):
        row = rows_ref[k : k + 1, :]
        upper = (row >= half).astype(jnp.int32)
        place = (upper * (half_all - half) + band_of * half + row).astype(F32)
        hots.append(hot_rows(as_column(place), 2 * half_all))
        hots_t.append(hot_columns(place, 2 * half_all))
    hot_t = jnp.concatenate(hots_t, 1)

    listed = jnp.concatenate(
        [jnp.broadcast_to(send_ref[0, d : d + 1, :], (bound, bound)) for d in range(8)], 0
    ).astype(F32)
    lane = lax.broadcasted_iota(jnp.int32, (8 * bound, bound), 1)
    line = lax.rem(lax.broadcasted_iota(jnp.int32, (8 * bound, bound), 0), bound)
    list_column = jnp.sum(jnp.where(lane == line, listed, 0.0), 1, keepdims=True)
    pick = hot_rows(list_column, mesh_rows)
    pick_t = hot_columns(as_row(list_column), mesh_rows)

    slot_copy.wait()
    slot_lines = jnp.concatenate(
        [
            jnp.broadcast_to(ref[k : k + 1, :], (half, 128))
            for ref in (slots_mine, slots_peer)
            for k in range(own_slots)
        ],
        0,
    ).astype(F32)
    shape = slot_lines.shape
    lane = lax.broadcasted_iota(jnp.int32, shape, 1)
    line = lax.rem(lax.broadcasted_iota(jnp.int32, shape, 0), half) + sub * half
    slot_column = jnp.sum(jnp.where(lane == line, slot_lines, 0.0), 1, keepdims=True)
    slot_hot = hot_rows(slot_column, table_rows)
    slot_hot_t = hot_columns(as_row(slot_column), table_rows)

    loads[7].wait()
    loads[8].wait()
    onward_1 = gather_finish(gather_1, gathered_mesh, 0)
    proj_mesh = dot_plain(gathered_mesh[...], enc_recv[...]).astype(BF16)
    for k in range(fanout):
        base = k * nodes
        pre_grid[base : base + nodes, :] = dot_plain(hots[k], proj_mesh)
        for at in range(0, nodes, CHUNK):
            here = slice(base + at, base + at + CHUNK)
            pre = pre_grid[here, :] + proj_grid[at : at + CHUNK, :]
            pre_grid[here, :] = pre
            hid[here, :] = (pre * jax.nn.sigmoid(pre)).astype(BF16)
        z_grid[base : base + nodes, :] = dot_plain(hid[base : base + nodes, :], enc_edge[...])
        for at in range(base, base + nodes, CHUNK):
            here = slice(at, at + CHUNK)
            normed, inverse = norm_parts(z_grid[here, :])
            z_grid[here, :] = normed
            inv_grid[here, :] = inverse
            hid[here, :] = normed.astype(BF16)

    def scatter_sum(values, mine, out, inbound, out_lat, in_lat, n_sub, n_lat, meanwhile):
        total = dot_plain(hot_t, values)
        low, high = total[0:half_all, :], total[half_all:, :]
        out[...] = jnp.where(sub == 0, high, low).astype(BF16)
        copy = to_sub(out, inbound, n_sub)
        copy.start()
        mine[...] = jnp.where(sub == 0, low, high)
        meanwhile()
        copy.wait()
        copies = []
        for step in range(bands - 1, 0, -1):
            rows = band_rows(lat_peer(step))
            out_lat[rows, :] = (mine[rows, :] + inbound[rows, :].astype(F32)).astype(BF16)
            copy = to_lat(out_lat.at[rows], in_lat.at[step], n_lat, step)
            copy.start()
            copies.append(copy)
        rows = band_rows(lat)
        own = mine[rows, :] + inbound[rows, :].astype(F32)
        return own, copies

    def scatter_finish(own, copies, in_lat):
        for copy in copies:
            copy.wait()
        for step in range(1, bands):
            own = own + in_lat[step].astype(F32)
        return own

    def slope_of(ref, start, stop):
        for at in range(start, stop, CHUNK):
            ref[at : at + CHUNK, :] = silu_slope(ref[at : at + CHUNK, :])

    own, copies = scatter_sum(
        hid[...], part_mine, part_out, part_in, lat_out, lat_in, 1, 1, lambda: None
    )
    slope_of(pre_grid, 0, fanout * nodes)
    for n in (10, 11, 12, 13, 14, 15, 16):
        loads[n].wait()
    bias_mesh = bias_mesh_ref[...].reshape(1, width)
    node_gain = node_gain_ref[...].reshape(1, width)
    mesh_gain = mesh_gain_ref[...].reshape(1, width)
    agg_grid = scatter_finish(own, copies, lat_in)

    agg_grid_normed, agg_grid_inverse = norm_parts(agg_grid)
    mid_half = (mesh_ref[my_rows, :].astype(F32) + agg_grid_normed * node_gain).astype(BF16)
    mid_full[my_rows, :] = mid_half
    mid_copy = to_sub(mid_full.at[my_rows], mid_full.at[my_rows], 2)
    mid_copy.start()
    recv_half = dot_plain(mid_half, proc_recv[...]).astype(BF16).astype(F32) + bias_mesh
    mid_copy.wait()
    send_mesh = dot_plain(mid_full[...], proc_send[...]).astype(BF16)
    bound_out[...] = dot_plain(pick, send_mesh).astype(BF16)

    def block_of(d):
        return pl.ds(d * bound, bound)

    def table_of(d):
        return pl.ds(mesh_rows + d * bound, bound)

    def to_near(source, target, n, d, sign):
        return pltpu.make_async_remote_copy(
            src_ref=source,
            dst_ref=target,
            send_sem=nb_s.at[n, d],
            recv_sem=nb_r.at[n, d],
            device_id=neighbour(d, sign),
            device_id_type=MESH,
        )

    for d in range(8):
        @pl.when(reaches(d))
        def _():
            to_near(bound_out.at[block_of(d)], table.at[table_of(d)], 0, d, 1).start()
    table[0:mesh_rows, :] = send_mesh
    for d in range(8):
        copy = to_near(bound_out.at[block_of(d)], table.at[table_of(d)], 0, d, 1)

        @pl.when(comes_from(d))
        def _():
            copy.wait_recv()

    edges = edges_half * half
    pre_mesh[...] = dot_plain(slot_hot, table[...])
    for at in range(0, edges, half):
        here = slice(at, at + half)
        pre = pre_mesh[here, :] + recv_half
        pre_mesh[here, :] = pre
        hid[here, :] = (pre * jax.nn.sigmoid(pre)).astype(BF16)
    z_mesh[...] = dot_plain(hid[0:edges, :], proc_edge[...])
    agg_mesh = jnp.zeros((half, width), F32)
    inverses = []
    for at in range(0, edges, half):
        here = slice(at, at + half)
        normed, inverse = norm_parts(z_mesh[here, :])
        z_mesh[here, :] = normed
        inverses.append(inverse)
        agg_mesh = agg_mesh + normed

    agg_mesh_normed, agg_mesh_inverse = norm_parts(agg_mesh)
    out_half = (mid_half.astype(F32) + agg_mesh_normed * mesh_gain).astype(BF16)
    out_half_mine[...] = out_half
    mesh_out_ref[my_rows, :] = out_half
    out_copy = to_sub(out_half_mine, out_half_peer, 3)
    out_copy.start()

    upstream = cot_ref[my_rows, :].astype(F32)
    d_agg_mesh = norm_back(agg_mesh_normed, agg_mesh_inverse, upstream * mesh_gain)
    for n, at in enumerate(range(0, edges, half)):
        here = slice(at, at + half)
        hid[here, :] = norm_back(z_mesh[here, :], inverses[n], d_agg_mesh).astype(BF16)
    work[0:edges, :] = dot_trans(hid[0:edges, :], proc_edge[...])
    d_recv = jnp.zeros((half, width), F32)
    for at in range(0, edges, half):
        here = slice(at, at + half)
        d_pre = (work[here, :] * silu_slope(pre_mesh[here, :])).astype(BF16)
        hid[here, :] = d_pre
        d_recv = d_recv + d_pre.astype(F32)
    d_table = dot_plain(slot_hot_t, hid[0:edges, :])
    back_out[...] = d_table[mesh_rows : mesh_rows + 8 * bound, :].astype(BF16)
    for d in range(8):
        @pl.when(comes_from(d))
        def _():
            to_near(back_out.at[block_of(d)], back_in.at[block_of(d)], 1, d, -1).start()
    d_mid = upstream + dot_trans(d_recv.astype(BF16), proc_recv[...])
    for d in range(8):
        copy = to_near(back_out.at[block_of(d)], back_in.at[block_of(d)], 1, d, -1)

        @pl.when(reaches(d))
        def _():
            copy.wait_recv()
    d_send = d_table[0:mesh_rows, :] + dot_plain(pick_t, back_in[...])
    send_part_out[...] = jnp.where(sub == 0, d_send[half:, :], d_send[0:half, :])
    send_copy = to_sub(send_part_out, send_part_in, 4)
    send_copy.start()
    d_send_half = jnp.where(sub == 0, d_send[0:half, :], d_send[half:, :])
    send_copy.wait()
    d_send_half = d_send_half + send_part_in[...]
    d_mid = d_mid + dot_trans(d_send_half.astype(BF16), proc_send[...])
    d_agg_grid = norm_back(agg_grid_normed, agg_grid_inverse, d_mid * node_gain)
    d_agg_all[half_rows(sub, lat), :] = d_agg_grid.astype(BF16)
    own_copy = to_sub(d_agg_all.at[half_rows(sub, lat)], d_agg_all.at[half_rows(sub, lat)], 5)
    own_copy.start()
    gather_2 = gather_start(d_agg_all.at[half_rows(sub, lat)], d_agg_all, 2)
    out_copy.wait()
    mesh_out_ref[peer_rows, :] = out_half_peer[...]
    onward_2 = gather_finish(gather_2, d_agg_all, 1)
    own_copy.wait()

    for k in range(fanout):
        base = k * nodes
        work[base : base + nodes, :] = dot_plain(hots[k], d_agg_all[...])
        for at in range(base, base + nodes, CHUNK):
            here = slice(at, at + CHUNK)
            hid[here, :] = norm_back(z_grid[here, :], inv_grid[here, :], work[here, :]).astype(BF16)
        work[base : base + nodes, :] = dot_trans(hid[base : base + nodes, :], enc_edge[...])
        for at in range(base, base + nodes, CHUNK):
            here = slice(at, at + CHUNK)
            hid[here, :] = (work[here, :] * pre_grid[here, :]).astype(BF16)

    def grid_side():
        total = hid[0:nodes, :].astype(F32)
        for k in range(1, fanout):
            total = total + hid[k * nodes : (k + 1) * nodes, :].astype(F32)
        grid_grad_ref[...] = dot_trans(total.astype(BF16), enc_send[...]).astype(BF16)

    own, copies_2 = scatter_sum(
        hid[...], part_mine, part_out_2, part_in_2, lat_out_2, lat_in_2, 6, 3, lambda: None
    )
    grid_side()
    d_proj_mesh = scatter_finish(own, copies_2, lat_in_2)
    grad_half = (d_mid + dot_trans(d_proj_mesh.astype(BF16), enc_recv[...])).astype(BF16)
    grad_half_mine[...] = grad_half
    grad_copy = to_sub(grad_half_mine, grad_half_peer, 7)
    grad_copy.start()
    mesh_grad_ref[my_rows, :] = grad_half
    for copy in gather_1 + gather_2 + onward_1 + onward_2:
        copy.wait_send()
    for d in range(8):
        @pl.when(reaches(d))
        def _():
            to_near(bound_out.at[block_of(d)], table.at[table_of(d)], 0, d, 1).wait_send()

        @pl.when(comes_from(d))
        def _():
            to_near(back_out.at[block_of(d)], back_in.at[block_of(d)], 1, d, -1).wait_send()
    grad_copy.wait()
    mesh_grad_ref[peer_rows, :] = grad_half_peer[...]


def store_kernel(a, b, c, a_out, b_out, c_out, sems):
    copies = [
        pltpu.make_async_copy(source, target, sems.at[n])
        for n, (source, target) in enumerate(((a, a_out), (b, b_out), (c, c_out)))
    ]
    for copy in copies:
        copy.start()
    for copy in copies:
        copy.wait()


def on_device(bands, sectors, *args):
    args = list(args)
    for n in (1, 2, 4):
        args[n] = args[n].T
    grid_latent, mesh_latent, mesh_slots = args[0], args[3], args[4]
    send_rows, edge_rows = args[5], args[2]
    nodes, width = grid_latent.shape
    mesh_rows = mesh_latent.shape[0]
    half = mesh_rows // 2
    bound = 8 * send_rows.shape[2]
    table_rows = -(-(mesh_rows + bound) // 128) * 128
    edges = edge_rows.shape[0] * nodes
    mesh_edges = 2 * mesh_slots.shape[0] * half
    every = bands * mesh_rows
    most = max(edges, mesh_edges)
    vmem = pl.BlockSpec(memory_space=pltpu.VMEM)
    hbm = pl.BlockSpec(memory_space=pltpu.HBM)
    dma = pltpu.SemaphoreType.DMA
    out_shape = (
        jax.ShapeDtypeStruct((mesh_rows, width), BF16),
        jax.ShapeDtypeStruct((mesh_rows, width), BF16),
        jax.ShapeDtypeStruct((nodes, width), BF16),
    )
    results = pl.pallas_call(
        functools.partial(kernel, bands, sectors),
        out_shape=out_shape,
        in_specs=[hbm] * len(args),
        out_specs=(vmem, vmem, vmem),
        scratch_shapes=[pltpu.VMEM(a.shape, a.dtype) for a in args]
        + [
            pltpu.VMEM((8, 128), jnp.int32),
            pltpu.VMEM((8, 128), jnp.int32),
            pltpu.VMEM((every, width), BF16),
            pltpu.VMEM((nodes, width), F32),
            pltpu.VMEM((edges, width), F32),
            pltpu.VMEM((edges, width), F32),
            pltpu.VMEM((edges, 1), F32),
            pltpu.VMEM((most, width), BF16),
            pltpu.VMEM((most, width), F32),
            pltpu.VMEM((every // 2, width), F32),
            pltpu.VMEM((every // 2, width), BF16),
            pltpu.VMEM((every // 2, width), BF16),
            pltpu.VMEM((every // 2, width), BF16),
            pltpu.VMEM((bands, half, width), BF16),
            pltpu.VMEM((mesh_rows, width), BF16),
            pltpu.VMEM((bound, width), BF16),
            pltpu.VMEM((table_rows, width), BF16),
            pltpu.VMEM((mesh_edges, width), F32),
            pltpu.VMEM((mesh_edges, width), F32),
            pltpu.VMEM((half, width), BF16),
            pltpu.VMEM((half, width), BF16),
            pltpu.VMEM((bound, width), BF16),
            pltpu.VMEM((bound, width), BF16),
            pltpu.VMEM((half, width), F32),
            pltpu.VMEM((half, width), F32),
            pltpu.VMEM((every, width), BF16),
            pltpu.VMEM((every // 2, width), BF16),
            pltpu.VMEM((every // 2, width), BF16),
            pltpu.VMEM((every // 2, width), BF16),
            pltpu.VMEM((bands, half, width), BF16),
            pltpu.VMEM((half, width), BF16),
            pltpu.VMEM((half, width), BF16),
            dma((17,)),
            dma((4, bands)),
            dma((4, bands)),
            dma((2, bands)),
            dma((2, bands)),
            dma((8,)),
            dma((8,)),
            dma((2, 8)),
            dma((2, 8)),
        ],
        compiler_params=pltpu.CompilerParams(
            collective_id=0, has_side_effects=True, vmem_limit_bytes=63 * 1024 * 1024 + 512 * 1024
        ),
    )(*args)
    return pl.pallas_call(
        store_kernel,
        out_shape=out_shape,
        in_specs=[vmem] * 3,
        out_specs=[hbm] * 3,
        scratch_shapes=[dma((3,))],
    )(*results)


def solution(mesh):
    part = P(("group", "lat", "lon"), None)
    node = P(("group", "lat", "lon", "sub"), None)
    placed = (
        (node, node, node, part, P(("group", "lat", "lon"), "sub"))
        + (P(("group", "lat", "lon"), None, None),)
        + (P(),) * 10
        + (part,)
    )
    return jax.shard_map(
        functools.partial(on_device, mesh.shape["lat"], mesh.shape["lon"]),
        mesh=mesh,
        in_specs=placed,
        out_specs=(part, part, node),
        check_vma=False,
    )
```

```python
import functools

import jax
import jax.numpy as jnp
from jax import lax
from jax.experimental import pallas as pl
from jax.experimental.pallas import tpu as pltpu
from jax.sharding import PartitionSpec as P

EPS = 1e-05
DIRECTIONS = ((-1, -1), (-1, 0), (-1, 1), (0, -1), (0, 1), (1, -1), (1, 0), (1, 1))
ORDER = (0, 2, 1, 3, 4, 5, 7, 6)
MESH = pl.DeviceIdType.MESH
F32 = jnp.float32
BF16 = jnp.bfloat16
CHUNK = 64


def dot_plain(left, right):
    return jnp.dot(left, right, preferred_element_type=F32)


def dot_trans(left, right):
    return lax.dot_general(left, right, (((1,), (1,)), ((), ())), preferred_element_type=F32)


def row_mean(value):
    return jnp.mean(value, -1, keepdims=True)


def norm_parts(value):
    centred = value - row_mean(value)
    inverse = lax.rsqrt(row_mean(centred * centred) + EPS)
    return centred * inverse, inverse


def norm_back(normed, inverse, upstream):
    inner = row_mean(upstream * normed)
    return (upstream - row_mean(upstream) - normed * inner) * inverse


def silu_slope(value):
    sigma = jax.nn.sigmoid(value)
    return sigma * (1.0 + value * (1.0 - sigma))


def iota_f32(shape, axis):
    return lax.broadcasted_iota(jnp.int32, shape, axis).astype(F32)


def as_row(column):
    n = column.shape[0]
    shape = (n, n)
    same = lax.broadcasted_iota(jnp.int32, shape, 0) == lax.broadcasted_iota(jnp.int32, shape, 1)
    return jnp.sum(jnp.where(same, column, 0.0), 0, keepdims=True)


def as_column(row):
    n = row.shape[1]
    shape = (n, n)
    same = lax.broadcasted_iota(jnp.int32, shape, 0) == lax.broadcasted_iota(jnp.int32, shape, 1)
    return jnp.sum(jnp.where(same, row, 0.0), 1, keepdims=True)


def hot_rows(column, count):
    return (column == iota_f32((column.shape[0], count), 1)).astype(F32).astype(BF16)


def hot_columns(row, count):
    return (row == iota_f32((count, row.shape[1]), 0)).astype(F32).astype(BF16)


def kernel(
    bands,
    sectors,
    *refs,
):
    inputs, outputs, local = refs[:17], refs[17:20], refs[20:40]
    body(bands, sectors, inputs, outputs, *local, *refs[40:])


def body(
    bands,
    sectors,
    inputs,
    outputs,
    grid_ref,
    band_ref,
    rows_ref,
    mesh_ref,
    slots_ref,
    send_ref,
    enc_send,
    enc_recv,
    enc_edge,
    bias_grid_ref,
    node_gain_ref,
    proc_send,
    proc_recv,
    proc_edge,
    bias_mesh_ref,
    mesh_gain_ref,
    cot_ref,
    mesh_out_ref,
    mesh_grad_ref,
    grid_grad_ref,
    slots_mine,
    slots_peer,
    gathered_mesh,
    proj_grid,
    pre_grid,
    z_grid,
    inv_grid,
    hid,
    work,
    part_mine,
    part_out,
    part_in,
    lat_out,
    lat_in,
    mid_full,
    bound_out,
    table,
    pre_mesh,
    z_mesh,
    out_half_peer,
    out_half_mine,
    back_out,
    back_in,
    send_part_out,
    send_part_in,
    d_agg_all,
    part_out_2,
    part_in_2,
    lat_out_2,
    lat_in_2,
    grad_half_mine,
    grad_half_peer,
    w_sem,
    lat_s,
    lat_r,
    fwd_s,
    fwd_r,
    sub_s,
    sub_r,
    nb_s,
    nb_r,
    hot_t,
    chunk_s,
    chunk_r,
):
    lat, lon, sub = lax.axis_index("lat"), lax.axis_index("lon"), lax.axis_index("sub")
    other = 1 - sub
    nodes, width = grid_ref.shape
    fanout = rows_ref.shape[0]
    mesh_rows = mesh_ref.shape[0]
    half = mesh_rows // 2
    half_all = bands * half
    bound = send_ref.shape[2]
    own_slots = slots_ref.shape[0]
    edges_half = 2 * own_slots
    table_rows = table.shape[0]

    slots_mine[...] = jnp.zeros_like(slots_mine)
    table[mesh_rows:, :] = jnp.zeros((table_rows - mesh_rows, width), BF16)
    back_in[...] = jnp.zeros_like(back_in)

    barrier = pltpu.get_barrier_semaphore()

    def lat_peer(step):
        return lax.rem(lat + step, bands)

    def reaches(d):
        target = lat + DIRECTIONS[d][0]
        return (target >= 0) & (target < bands)

    def comes_from(d):
        target = lat - DIRECTIONS[d][0]
        return (target >= 0) & (target < bands)

    def neighbour(d, sign):
        return {
            "lat": lat + sign * DIRECTIONS[d][0],
            "lon": lax.rem(lon + sign * DIRECTIONS[d][1] + sectors, sectors),
        }

    for step in range(1, bands):
        pl.semaphore_signal(barrier, inc=1, device_id={"lat": lat_peer(step)}, device_id_type=MESH)
    pl.semaphore_signal(barrier, inc=1, device_id={"sub": other}, device_id_type=MESH)
    diagonal = [d for d in range(8) if DIRECTIONS[d][1] != 0]
    for d in diagonal:
        @pl.when(reaches(d))
        def _():
            pl.semaphore_signal(barrier, inc=1, device_id=neighbour(d, 1), device_id_type=MESH)

    places = (
        grid_ref, band_ref, rows_ref, mesh_ref, slots_ref, send_ref, enc_send, enc_recv, enc_edge,
        bias_grid_ref, node_gain_ref, proc_send, proc_recv, proc_edge, bias_mesh_ref,
        mesh_gain_ref, cot_ref,
    )
    loads = [
        pltpu.make_async_copy(a, b, w_sem.at[n]) for n, (a, b) in enumerate(zip(inputs, places))
    ]
    early = (3, 4, 0, 6, 1, 2, 5)
    for n in early + tuple(n for n in range(17) if n not in early):
        loads[n].start()

    stores = [
        pltpu.make_async_copy(a, b, w_sem.at[17 + n])
        for n, (a, b) in enumerate(zip((mesh_out_ref, mesh_grad_ref, grid_grad_ref), outputs))
    ]
    near = 2 + 2 * (lat > 0).astype(jnp.int32) + 2 * (lat < bands - 1).astype(jnp.int32)
    loads[3].wait()
    loads[4].wait()
    slots_mine[0:own_slots, 0:mesh_rows] = slots_ref[...]
    pl.semaphore_wait(barrier, bands + near)

    def half_rows(which, band):
        return pl.ds(pl.multiple_of(which * half_all + band * half, half), half)

    def band_rows(band):
        return pl.ds(pl.multiple_of(band * half, half), half)

    def all_half(which):
        return pl.ds(pl.multiple_of(which * half_all, half_all), half_all)

    my_rows = pl.ds(pl.multiple_of(sub * half, half), half)
    peer_rows = pl.ds(pl.multiple_of(other * half, half), half)

    def to_sub(source, target, n):
        return pltpu.make_async_remote_copy(
            src_ref=source,
            dst_ref=target,
            send_sem=sub_s.at[n],
            recv_sem=sub_r.at[n],
            device_id={"sub": other},
            device_id_type=MESH,
        )

    def to_lat(source, target, n, step):
        return pltpu.make_async_remote_copy(
            src_ref=source,
            dst_ref=target,
            send_sem=lat_s.at[n, step],
            recv_sem=lat_r.at[n, step],
            device_id={"lat": lat_peer(step)},
            device_id_type=MESH,
        )

    def gather_start(source, whole, n):
        copies = []
        for step in range(1, bands):
            copy = to_lat(source, whole.at[half_rows(sub, lat)], n, step)
            copy.start()
            copies.append(copy)
        return copies

    def gather_finish(copies, whole, n):
        onward = []
        for step in range(1, bands):
            copies[step - 1].wait_recv()
            origin = lax.rem(lat - step + bands, bands)
            copy = pltpu.make_async_remote_copy(
                src_ref=whole.at[half_rows(sub, origin)],
                dst_ref=whole.at[half_rows(sub, origin)],
                send_sem=fwd_s.at[n, step],
                recv_sem=fwd_r.at[n, step],
                device_id={"sub": other},
                device_id_type=MESH,
            )
            copy.start()
            onward.append(copy)
        for copy in onward:
            copy.wait_recv()
        return onward

    slot_copy = to_sub(slots_mine, slots_peer, 0)
    slot_copy.start()
    gather_1 = gather_start(mesh_ref.at[my_rows], gathered_mesh, 0)
    gathered_mesh[half_rows(0, lat), :] = mesh_ref[0:half, :]
    gathered_mesh[half_rows(1, lat), :] = mesh_ref[half:, :]

    for n in (0, 6, 9):
        loads[n].wait()
    bias_grid = bias_grid_ref[...].reshape(1, width)
    proj_grid[...] = (dot_plain(grid_ref[...], enc_send[...])).astype(BF16).astype(F32) + bias_grid

    for n in (1, 2, 5):
        loads[n].wait()
    band_of = band_ref[...]
    hots, hots_t = [], []
    for k in range(fanout):
        row = rows_ref[k : k + 1, :]
        upper = (row >= half).astype(jnp.int32)
        place = (upper * (half_all - half) + band_of * half + row).astype(F32)
        hots.append(hot_rows(as_column(place), 2 * half_all))
        hots_t.append(hot_columns(place, 2 * half_all))
    hot_t[...] = jnp.concatenate(hots_t, 1)

    listed = jnp.concatenate(
        [jnp.broadcast_to(send_ref[0, d : d + 1, :], (bound, bound)) for d in ORDER], 0
    ).astype(F32)
    lane = lax.broadcasted_iota(jnp.int32, (8 * bound, bound), 1)
    line = lax.rem(lax.broadcasted_iota(jnp.int32, (8 * bound, bound), 0), bound)
    list_column = jnp.sum(jnp.where(lane == line, listed, 0.0), 1, keepdims=True)
    pick = hot_rows(list_column, mesh_rows)
    pick_t = hot_columns(as_row(list_column), mesh_rows)

    slot_copy.wait()
    slot_lines = jnp.concatenate(
        [
            jnp.broadcast_to(ref[k : k + 1, :], (half, 128))
            for ref in (slots_mine, slots_peer)
            for k in range(own_slots)
        ],
        0,
    ).astype(F32)
    shape = slot_lines.shape
    lane = lax.broadcasted_iota(jnp.int32, shape, 1)
    line = lax.rem(lax.broadcasted_iota(jnp.int32, shape, 0), half) + sub * half
    slot_raw = slot_column = jnp.sum(jnp.where(lane == line, slot_lines, 0.0), 1, keepdims=True)
    for d, move in ((1, bound), (2, -bound), (6, bound), (7, -bound)):
        first = mesh_rows + d * bound
        inside = (slot_raw >= first) & (slot_raw < first + bound)
        slot_column = slot_column + jnp.where(inside, float(move), 0.0)
    slot_hot = hot_rows(slot_column, table_rows)
    slot_hot_t = hot_columns(as_row(slot_column), table_rows)

    loads[7].wait()
    loads[8].wait()
    onward_1 = gather_finish(gather_1, gathered_mesh, 0)
    proj_mesh = dot_plain(gathered_mesh[...], enc_recv[...]).astype(BF16)
    for k in range(fanout):
        base = k * nodes
        pre_grid[base : base + nodes, :] = dot_plain(hots[k], proj_mesh)
        for at in range(0, nodes, CHUNK):
            here = slice(base + at, base + at + CHUNK)
            pre = pre_grid[here, :] + proj_grid[at : at + CHUNK, :]
            pre_grid[here, :] = pre
            hid[here, :] = (pre * jax.nn.sigmoid(pre)).astype(BF16)
        z_grid[base : base + nodes, :] = dot_plain(hid[base : base + nodes, :], enc_edge[...])
        for at in range(base, base + nodes, CHUNK):
            here = slice(at, at + CHUNK)
            normed, inverse = norm_parts(z_grid[here, :])
            z_grid[here, :] = normed
            inv_grid[here, :] = inverse
            hid[here, :] = normed.astype(BF16)

    def scatter_sum(values, mine, out, inbound, out_lat, in_lat, n_sub, n_lat):
        out[...] = dot_plain(hot_t[all_half(other), :], values).astype(BF16)
        order = list(range(1, bands)) + [0]
        across = []
        for step in order:
            rows = band_rows(lat_peer(step))
            copy = pltpu.make_async_remote_copy(
                src_ref=out.at[rows],
                dst_ref=inbound.at[rows],
                send_sem=chunk_s.at[n_sub, step],
                recv_sem=chunk_r.at[n_sub, step],
                device_id={"sub": other},
                device_id_type=MESH,
            )
            copy.start()
            across.append(copy)
        mine[...] = dot_plain(hot_t[all_half(sub), :], values)
        copies = []
        for copy, step in zip(across, order):
            copy.wait()
            if step == 0:
                continue
            rows = band_rows(lat_peer(step))
            out_lat[rows, :] = (mine[rows, :] + inbound[rows, :].astype(F32)).astype(BF16)
            copy = to_lat(out_lat.at[rows], in_lat.at[step], n_lat, step)
            copy.start()
            copies.append(copy)
        rows = band_rows(lat)
        own = mine[rows, :] + inbound[rows, :].astype(F32)
        return own, copies

    def scatter_finish(own, copies, in_lat):
        for copy in copies:
            copy.wait()
        for step in range(1, bands):
            own = own + in_lat[step].astype(F32)
        return own

    def slope_of(ref, start, stop):
        for at in range(start, stop, CHUNK):
            ref[at : at + CHUNK, :] = silu_slope(ref[at : at + CHUNK, :])

    own, copies = scatter_sum(
        hid[...], part_mine, part_out, part_in, lat_out, lat_in, 0, 1
    )
    slope_of(pre_grid, 0, fanout * nodes)
    for n in (10, 11, 12, 13, 14, 15, 16):
        loads[n].wait()
    bias_mesh = bias_mesh_ref[...].reshape(1, width)
    node_gain = node_gain_ref[...].reshape(1, width)
    mesh_gain = mesh_gain_ref[...].reshape(1, width)
    agg_grid = scatter_finish(own, copies, lat_in)

    agg_grid_normed, agg_grid_inverse = norm_parts(agg_grid)
    mid_half = (mesh_ref[my_rows, :].astype(F32) + agg_grid_normed * node_gain).astype(BF16)
    mid_full[my_rows, :] = mid_half
    mid_copy = to_sub(mid_full.at[my_rows], mid_full.at[my_rows], 2)
    mid_copy.start()
    recv_half = dot_plain(mid_half, proc_recv[...]).astype(BF16).astype(F32) + bias_mesh
    mid_copy.wait()
    send_mesh = dot_plain(mid_full[...], proc_send[...]).astype(BF16)
    bound_out[...] = dot_plain(pick, send_mesh).astype(BF16)

    if sectors == 2:
        runs = ((0, 2), (2, 1), (3, 2), (5, 2), (7, 1))
    else:
        runs = tuple((at, 1) for at in range(8))

    def block_of(run):
        return pl.ds(run[0] * bound, run[1] * bound)

    def table_of(run):
        return pl.ds(mesh_rows + run[0] * bound, run[1] * bound)

    def to_near(source, target, n, run, sign):
        return pltpu.make_async_remote_copy(
            src_ref=source,
            dst_ref=target,
            send_sem=nb_s.at[n, run[0]],
            recv_sem=nb_r.at[n, run[0]],
            device_id=neighbour(ORDER[run[0]], sign),
            device_id_type=MESH,
        )

    for d in runs:
        @pl.when(reaches(ORDER[d[0]]))
        def _():
            to_near(bound_out.at[block_of(d)], table.at[table_of(d)], 0, d, 1).start()
    table[0:mesh_rows, :] = send_mesh
    for d in runs:
        copy = to_near(bound_out.at[block_of(d)], table.at[table_of(d)], 0, d, 1)

        @pl.when(comes_from(ORDER[d[0]]))
        def _():
            copy.wait_recv()

    edges = edges_half * half
    pre_mesh[...] = dot_plain(slot_hot, table[...])
    for at in range(0, edges, half):
        here = slice(at, at + half)
        pre = pre_mesh[here, :] + recv_half
        pre_mesh[here, :] = pre
        hid[here, :] = (pre * jax.nn.sigmoid(pre)).astype(BF16)
    z_mesh[...] = dot_plain(hid[0:edges, :], proc_edge[...])
    agg_mesh = jnp.zeros((half, width), F32)
    inverses = []
    for at in range(0, edges, half):
        here = slice(at, at + half)
        normed, inverse = norm_parts(z_mesh[here, :])
        z_mesh[here, :] = normed
        inverses.append(inverse)
        agg_mesh = agg_mesh + normed

    agg_mesh_normed, agg_mesh_inverse = norm_parts(agg_mesh)
    out_half = (mid_half.astype(F32) + agg_mesh_normed * mesh_gain).astype(BF16)
    out_half_mine[...] = out_half
    mesh_out_ref[my_rows, :] = out_half
    out_copy = to_sub(out_half_mine, out_half_peer, 3)
    out_copy.start()

    upstream = cot_ref[my_rows, :].astype(F32)
    d_agg_mesh = norm_back(agg_mesh_normed, agg_mesh_inverse, upstream * mesh_gain)
    for n, at in enumerate(range(0, edges, half)):
        here = slice(at, at + half)
        hid[here, :] = norm_back(z_mesh[here, :], inverses[n], d_agg_mesh).astype(BF16)
    work[0:edges, :] = dot_trans(hid[0:edges, :], proc_edge[...])
    d_recv = jnp.zeros((half, width), F32)
    for at in range(0, edges, half):
        here = slice(at, at + half)
        d_pre = (work[here, :] * silu_slope(pre_mesh[here, :])).astype(BF16)
        hid[here, :] = d_pre
        d_recv = d_recv + d_pre.astype(F32)
    d_table = dot_plain(slot_hot_t, hid[0:edges, :])
    back_out[...] = d_table[mesh_rows : mesh_rows + 8 * bound, :].astype(BF16)
    for d in runs:
        @pl.when(comes_from(ORDER[d[0]]))
        def _():
            to_near(back_out.at[block_of(d)], back_in.at[block_of(d)], 1, d, -1).start()
    d_mid = upstream + dot_trans(d_recv.astype(BF16), proc_recv[...])
    for d in runs:
        copy = to_near(back_out.at[block_of(d)], back_in.at[block_of(d)], 1, d, -1)

        @pl.when(reaches(ORDER[d[0]]))
        def _():
            copy.wait_recv()
    d_send = d_table[0:mesh_rows, :] + dot_plain(pick_t, back_in[...])
    send_part_out[...] = jnp.where(sub == 0, d_send[half:, :], d_send[0:half, :])
    send_copy = to_sub(send_part_out, send_part_in, 4)
    send_copy.start()
    d_send_half = jnp.where(sub == 0, d_send[0:half, :], d_send[half:, :])
    send_copy.wait()
    d_send_half = d_send_half + send_part_in[...]
    d_mid = d_mid + dot_trans(d_send_half.astype(BF16), proc_send[...])
    d_agg_grid = norm_back(agg_grid_normed, agg_grid_inverse, d_mid * node_gain)
    d_agg_all[half_rows(sub, lat), :] = d_agg_grid.astype(BF16)
    own_copy = to_sub(d_agg_all.at[half_rows(sub, lat)], d_agg_all.at[half_rows(sub, lat)], 5)
    own_copy.start()
    gather_2 = gather_start(d_agg_all.at[half_rows(sub, lat)], d_agg_all, 2)
    out_copy.wait()
    mesh_out_ref[peer_rows, :] = out_half_peer[...]
    stores[0].start()
    onward_2 = gather_finish(gather_2, d_agg_all, 1)
    own_copy.wait()

    for k in range(fanout):
        base = k * nodes
        work[base : base + nodes, :] = dot_plain(hots[k], d_agg_all[...])
        for at in range(base, base + nodes, CHUNK):
            here = slice(at, at + CHUNK)
            hid[here, :] = norm_back(z_grid[here, :], inv_grid[here, :], work[here, :]).astype(BF16)
        work[base : base + nodes, :] = dot_trans(hid[base : base + nodes, :], enc_edge[...])
        for at in range(base, base + nodes, CHUNK):
            here = slice(at, at + CHUNK)
            hid[here, :] = (work[here, :] * pre_grid[here, :]).astype(BF16)

    def grid_side():
        total = hid[0:nodes, :].astype(F32)
        for k in range(1, fanout):
            total = total + hid[k * nodes : (k + 1) * nodes, :].astype(F32)
        grid_grad_ref[...] = dot_trans(total.astype(BF16), enc_send[...]).astype(BF16)
        stores[2].start()

    own, copies_2 = scatter_sum(
        hid[...], part_mine, part_out_2, part_in_2, lat_out_2, lat_in_2, 1, 3
    )
    grid_side()
    d_proj_mesh = scatter_finish(own, copies_2, lat_in_2)
    grad_half = (d_mid + dot_trans(d_proj_mesh.astype(BF16), enc_recv[...])).astype(BF16)
    grad_half_mine[...] = grad_half
    grad_copy = to_sub(grad_half_mine, grad_half_peer, 7)
    grad_copy.start()
    mesh_grad_ref[my_rows, :] = grad_half
    for copy in gather_1 + gather_2 + onward_1 + onward_2:
        copy.wait_send()
    for d in runs:
        @pl.when(reaches(ORDER[d[0]]))
        def _():
            to_near(bound_out.at[block_of(d)], table.at[table_of(d)], 0, d, 1).wait_send()

        @pl.when(comes_from(ORDER[d[0]]))
        def _():
            to_near(back_out.at[block_of(d)], back_in.at[block_of(d)], 1, d, -1).wait_send()
    grad_copy.wait()
    mesh_grad_ref[peer_rows, :] = grad_half_peer[...]
    stores[1].start()
    for store in stores:
        store.wait()


def store_kernel(a, b, c, a_out, b_out, c_out, sems):
    copies = [
        pltpu.make_async_copy(source, target, sems.at[n])
        for n, (source, target) in enumerate(((a, a_out), (b, b_out), (c, c_out)))
    ]
    for copy in copies:
        copy.start()
    for copy in copies:
        copy.wait()


def on_device(bands, sectors, *args):
    args = list(args)
    for n in (1, 2, 4):
        args[n] = args[n].T
    grid_latent, mesh_latent, mesh_slots = args[0], args[3], args[4]
    send_rows, edge_rows = args[5], args[2]
    nodes, width = grid_latent.shape
    mesh_rows = mesh_latent.shape[0]
    half = mesh_rows // 2
    bound = 8 * send_rows.shape[2]
    table_rows = -(-(mesh_rows + bound) // 128) * 128
    edges = edge_rows.shape[0] * nodes
    mesh_edges = 2 * mesh_slots.shape[0] * half
    every = bands * mesh_rows
    most = max(edges, mesh_edges)
    hbm = pl.BlockSpec(memory_space=pltpu.HBM)
    dma = pltpu.SemaphoreType.DMA
    out_shape = (
        jax.ShapeDtypeStruct((mesh_rows, width), BF16),
        jax.ShapeDtypeStruct((mesh_rows, width), BF16),
        jax.ShapeDtypeStruct((nodes, width), BF16),
    )
    results = pl.pallas_call(
        functools.partial(kernel, bands, sectors),
        out_shape=out_shape,
        in_specs=[hbm] * len(args),
        out_specs=(hbm, hbm, hbm),
        scratch_shapes=[pltpu.VMEM(a.shape, a.dtype) for a in (*args, *out_shape)]
        + [
            pltpu.VMEM((8, 128), jnp.int32),
            pltpu.VMEM((8, 128), jnp.int32),
            pltpu.VMEM((every, width), BF16),
            pltpu.VMEM((nodes, width), F32),
            pltpu.VMEM((edges, width), F32),
            pltpu.VMEM((edges, width), F32),
            pltpu.VMEM((edges, 1), F32),
            pltpu.VMEM((most, width), BF16),
            pltpu.VMEM((most, width), F32),
            pltpu.VMEM((every // 2, width), F32),
            pltpu.VMEM((every // 2, width), BF16),
            pltpu.VMEM((every // 2, width), BF16),
            pltpu.VMEM((every // 2, width), BF16),
            pltpu.VMEM((bands, half, width), BF16),
            pltpu.VMEM((mesh_rows, width), BF16),
            pltpu.VMEM((bound, width), BF16),
            pltpu.VMEM((table_rows, width), BF16),
            pltpu.VMEM((mesh_edges, width), F32),
            pltpu.VMEM((mesh_edges, width), F32),
            pltpu.VMEM((half, width), BF16),
            pltpu.VMEM((half, width), BF16),
            pltpu.VMEM((bound, width), BF16),
            pltpu.VMEM((bound, width), BF16),
            pltpu.VMEM((half, width), F32),
            pltpu.VMEM((half, width), F32),
            pltpu.VMEM((every, width), BF16),
            pltpu.VMEM((every // 2, width), BF16),
            pltpu.VMEM((every // 2, width), BF16),
            pltpu.VMEM((every // 2, width), BF16),
            pltpu.VMEM((bands, half, width), BF16),
            pltpu.VMEM((half, width), BF16),
            pltpu.VMEM((half, width), BF16),
            dma((20,)),
            dma((4, bands)),
            dma((4, bands)),
            dma((2, bands)),
            dma((2, bands)),
            dma((8,)),
            dma((8,)),
            dma((2, 8)),
            dma((2, 8)),
            pltpu.VMEM((every, edges), BF16),
            dma((2, bands)),
            dma((2, bands)),
        ],
        compiler_params=pltpu.CompilerParams(
            collective_id=0, has_side_effects=True, vmem_limit_bytes=63 * 1024 * 1024 + 512 * 1024
        ),
    )(*args)
    return pl.pallas_call(
        store_kernel,
        out_shape=out_shape,
        in_specs=[pl.BlockSpec(memory_space=pltpu.VMEM)] * 3,
        out_specs=[hbm] * 3,
        scratch_shapes=[dma((3,))],
    )(*results)


def solution(mesh):
    part = P(("group", "lat", "lon"), None)
    node = P(("group", "lat", "lon", "sub"), None)
    placed = (
        (node, node, node, part, P(("group", "lat", "lon"), "sub"))
        + (P(("group", "lat", "lon"), None, None),)
        + (P(),) * 10
        + (part,)
    )
    return jax.shard_map(
        functools.partial(on_device, mesh.shape["lat"], mesh.shape["lon"]),
        mesh=mesh,
        in_specs=placed,
        out_specs=(part, part, node),
        check_vma=False,
    )
```
